768 devices in a mesh: blk: 16 (over z_hi, y), pairs: 48 (over z_lo, x, core).
Axes of the slice: x: 4, y: 8, z: 12 (z_hi: 2, z_lo: 6; z = z_hi * 6 + z_lo), core: 2. Of those that a mesh axis runs over, the one named last changes fastest.
Arguments:
- amplitudes: bfloat16 [3072, 48, 4096], P(('blk', 'pairs')), may hold values from -6 to 6
- integrals: bfloat16 [1024, 48, 4096], P('blk', 'pairs'), may hold values from -0.013671875 to 0.013671875
- amp_pattern: int32 [16, 256], replicated, may hold values 0 or 1
- int_pattern: int32 [16, 256], replicated, may hold values 0 or 1
- slab_ids: int32 [48], replicated, may hold values from 0 to 255, as said below
- pair_window: int32 [2, 3072], replicated, may hold values from 0 to 199
Outputs:
- ladder: float32 [3072, 1024], P(('blk', 'pairs'))
The draws below stay inside these ranges and needn't reach their ends.
Inputs may be any that keep to these rules, and one draw needn't show every extreme that they name: `slab_ids`: the entries are distinct; 0 and 255 are always among them.
All inputs are finite; a program needn't handle non-finite values.
Results may differ from the reference program's by a relative error of at most 0.0003.
Values may be sent and summed in bfloat16 or wider, within the bound.
No kernel may reach another device: no remote copies, remote signals or barrier semaphores. Data moves between devices by JAX's collectives and lax.ppermute only.
A program may use at most 64 MiB of HBM per device.

```python
import jax
import jax.numpy as jnp

TILE = 64
NVT = 16
NOCC = 200
R_BLK = 64
OT = 4
SLAB = 48
NPAIR = 3072
NROW = 1024
N_BLK = 16


def draw_slab_ids(key, part):
    key = jax.random.fold_in(key, 7)
    count_all = NVT * NVT
    middle = jax.random.permutation(key, count_all - 2).astype(jnp.int32) + 1
    ends = jnp.array([0, count_all - 1], jnp.int32)
    chosen = jnp.concatenate([ends, middle[:SLAB - 2]])
    order = jax.random.permutation(jax.random.fold_in(key, 1), SLAB)
    return chosen[order]


def place_ends(entries, rng, low, high):
    spot = [jax.random.randint(jax.random.fold_in(rng, axis), (), 0, length) for axis, length in enumerate(entries.shape)]
    main_axis = entries.shape.index(max(entries.shape))
    beside = spot[:main_axis] + [(spot[main_axis] + 1) % entries.shape[main_axis]] + spot[main_axis + 1:]
    return entries.at[tuple(spot)].set(low).at[tuple(beside)].set(high)


def shard_levels(own_key, dims, cuts, smallest, top_value):
    def one(dim, blocks):
        draws = jax.random.uniform(jax.random.fold_in(jax.random.fold_in(own_key, 6), dim), (blocks,), jnp.float32, smallest / len(cuts), top_value / len(cuts))
        return jnp.repeat(jnp.exp(draws), dims[dim] // blocks).reshape((-1,) + (1,) * (len(dims) - dim - 1))

    loudness = one(*cuts[0])
    for cut in cuts[1:]:
        loudness = loudness * one(*cut)
    return loudness


def normal_values(stream_key, dims, deviation, bound, cuts=(), kind=jnp.bfloat16):
    entries = jax.random.normal(stream_key, dims, jnp.float32) * deviation
    if len(cuts) > 0:
        entries = shard_levels(stream_key, dims, cuts, -0.22, 0.18) * entries
    return jnp.clip(entries, min=-bound, max=bound).astype(kind)


def setup_inputs(seed: int = 0) -> dict:
    seeds = jax.random.split(jax.random.key(seed), 7)
    return {
        "amplitudes": normal_values(seeds[0], (NPAIR, SLAB, TILE * TILE), 1.0, 6.0, ((0, 768),)),
        "integrals": normal_values(seeds[1], (NROW, SLAB, TILE * TILE), (SLAB * TILE * TILE) ** -0.5, 0.013671875, ((0, 16), (1, 48))),
        "amp_pattern": place_ends((jax.random.randint(seeds[2], (OT * OT, NVT * NVT), 0, 4) < 3).astype(jnp.int32), jax.random.fold_in(seeds[2], 1), 0, 1),
        "int_pattern": place_ends((jax.random.randint(seeds[3], (NROW // TILE, NVT * NVT), 0, 4) < 3).astype(jnp.int32), jax.random.fold_in(seeds[3], 1), 0, 1),
        "slab_ids": draw_slab_ids(jax.random.fold_in(seeds[6], 71), 0),
        "pair_window": place_ends(jax.random.randint(seeds[5], (2, NPAIR), 0, NOCC), jax.random.fold_in(seeds[5], 1), 0, NOCC - 1).astype(jnp.int32),
    }


def reference(amplitudes, integrals, amp_pattern, int_pattern, slab_ids, pair_window):
    occ_tiles = (NOCC + TILE - 1) // TILE
    occ_tile = (pair_window[0] // TILE) * occ_tiles + pair_window[1] // TILE
    amp_mask = amp_pattern[occ_tile][:, slab_ids]
    row_tiles = jnp.arange(R_BLK * N_BLK, dtype=jnp.int32) // TILE
    int_mask = int_pattern[row_tiles][:, slab_ids]
    masked_amp = amplitudes * amp_mask[:, :, None].astype(amplitudes.dtype)
    masked_int = integrals * int_mask[:, :, None].astype(integrals.dtype)
    flat_amp = masked_amp.reshape(masked_amp.shape[0], -1)
    flat_int = masked_int.reshape(masked_int.shape[0], -1)
    return jnp.dot(flat_amp, flat_int.T, preferred_element_type=jnp.float32)
```

```python
import functools

import jax
import jax.numpy as jnp
from jax import lax
from jax.experimental import pallas as pl
from jax.experimental.pallas import tpu as pltpu
from jax.sharding import Mesh
from jax.sharding import PartitionSpec as P

TILE = 64
NOCC = 200
OT = (NOCC + TILE - 1) // TILE
ZH, Y, ZL, X, CORE = 2, 8, 6, 4, 2
PIECES = 2
ALL = ("zh", "y", "zl", "x", "c")


def onehot(index_list, width):
    return (index_list[:, None] == jnp.arange(width, dtype=jnp.int32)[None, :]).astype(jnp.bfloat16)


def split_rows(where_ref, slab_ref, pattern_ref, b_ref, *outs):
    slab = slab_ref[where_ref[1]]
    keep = pattern_ref[where_ref[0], slab].astype(jnp.float32).astype(jnp.bfloat16)
    rows = outs[0].shape[1]
    width = outs[0].shape[2]
    for piece, out in enumerate(outs):
        for y in range(Y):
            out[y] = b_ref[piece * rows : (piece + 1) * rows, y * width : (y + 1) * width] * keep


def ladder_piece(core_ref, a_ref, b_ref, mine_ref, other_ref, acc):
    step = pl.program_id(0)
    core = core_ref[0]
    half = b_ref.shape[2]

    @pl.when(step == 0)
    def _():
        acc[...] = jnp.zeros_like(acc)

    for t in range(2):
        a = a_ref[core if t == 0 else 1 - core]
        for zh in range(ZH):
            acc[t, :, zh * half : (zh + 1) * half] += lax.dot_general(
                a, b_ref[zh, 0], (((1,), (1,)), ((), ())), preferred_element_type=jnp.float32
            )

    @pl.when(step == ZL - 1)
    def _():
        columns = acc.shape[2] // 128
        chips = Y * X
        per = acc.shape[1] // chips
        for t, out in enumerate((mine_ref, other_ref)):
            for i in range(per):
                for k in range(columns):
                    out[pl.ds(i * columns + k, chips, stride=per * columns), :] = acc[
                        t, i * chips : (i + 1) * chips, k * 128 : (k + 1) * 128
                    ]


def per_device(amplitudes, integrals, amp_pattern, int_pattern, slab_ids, pair_window):
    zh, y, zl, x, c = (lax.axis_index(name) for name in ALL)
    block = zh * Y + y
    owner = (zl * X + x) * CORE + c
    pairs, slabs, depth = amplitudes.shape
    rows = integrals.shape[0]
    width = depth // Y
    part = rows // PIECES
    smem = pl.BlockSpec(memory_space=pltpu.SMEM)

    pieces = pl.pallas_call(
        split_rows,
        out_shape=[jax.ShapeDtypeStruct((Y, part, width), jnp.bfloat16)] * PIECES,
        in_specs=[smem, smem, smem, pl.BlockSpec(memory_space=pltpu.VMEM)],
        out_specs=[pl.BlockSpec(memory_space=pltpu.VMEM)] * PIECES,
    )(jnp.stack([block, owner]).astype(jnp.int32), slab_ids, int_pattern, integrals.reshape(rows, depth))

    spread = []
    gathered = []
    for piece in pieces:
        if spread:
            piece, _ = lax.optimization_barrier((piece, spread[-1]))
        moved = lax.all_to_all(piece, "y", 0, 0, tiled=True)
        spread.append(moved)
        gathered.append(lax.all_gather(moved.reshape(Y * part, width), ("zh", "zl"), axis=0, tiled=True))

    window = lax.dynamic_slice_in_dim(pair_window, (block * (ZL * X * CORE) + owner) * pairs, pairs, 1)
    occ_tile = window[0] // TILE * OT + window[1] // TILE
    picked = jnp.dot(onehot(occ_tile, amp_pattern.shape[0]), amp_pattern.astype(jnp.bfloat16))
    mask = jnp.dot(picked, onehot(slab_ids, amp_pattern.shape[1]).T)
    masked = amplitudes * mask[:, :, None]
    masked = masked.reshape(pairs, ZL, X * CORE, Y, width).transpose(3, 2, 0, 1, 4)
    masked = masked.reshape(Y * X * CORE, pairs * ZL, width)
    masked, _ = lax.optimization_barrier((masked, spread[-1]))
    swapped = lax.all_to_all(masked, ("y", "x", "c"), 0, 0, tiled=True)
    amps = swapped.reshape(Y * X, CORE, pairs, ZL, width).transpose(1, 2, 0, 3, 4)
    amps = amps.reshape(CORE, pairs * Y * X, ZL * width)

    core = c.reshape(1).astype(jnp.int32)
    cols = ZH * Y * part
    lines = cols // 128
    out_rows = Y * X * pairs * lines
    results = []
    for full in gathered:
        mine, other = pl.pallas_call(
            ladder_piece,
            grid=(ZL,),
            out_shape=[jax.ShapeDtypeStruct((out_rows, 128), jnp.float32)] * 2,
            in_specs=[
                smem,
                pl.BlockSpec((CORE, pairs * Y * X, width), lambda k: (0, 0, k)),
                pl.BlockSpec((ZH, 1, Y * part, width), lambda k: (0, k, 0, 0)),
            ],
            out_specs=[pl.BlockSpec((out_rows, 128), lambda k: (0, 0))] * 2,
            scratch_shapes=[pltpu.VMEM((2, pairs * Y * X, cols), jnp.float32)],
            compiler_params=pltpu.CompilerParams(
                dimension_semantics=("arbitrary",), vmem_limit_bytes=24 * 1024 * 1024
            ),
            cost_estimate=pl.CostEstimate(
                flops=4 * pairs * Y * X * cols * ZL * width,
                bytes_accessed=4 * 1024 * 1024,
                transcendentals=0,
            ),
        )(core, amps, full.reshape(ZH, ZL, Y * part, width))
        got = lax.ppermute(other, "c", [(0, 1), (1, 0)])
        summed = (mine + got).reshape(Y * X, pairs * lines, 128)
        sums = lax.all_to_all(summed, ("y", "x"), 0, 0, tiled=True)
        results.append(sums.sum(0).reshape(pairs, ZH * Y, part))
    return jnp.stack(results, axis=2).reshape(pairs, ZH * Y * rows)


def solution(mesh):
    fine = Mesh(mesh.devices.reshape(ZH, Y, ZL, X, CORE), ALL)
    first = ("zh", "y", "zl", "x", "c")
    placed = (P(first, None, None), P(("zh", "y"), ("zl", "x", "c"), None), P(), P(), P(), P())
    return jax.shard_map(per_device, mesh=fine, in_specs=placed, out_specs=P(first, None), check_vma=False)
```

```python
import functools

import jax
import jax.numpy as jnp
from jax import lax
from jax.experimental import pallas as pl
from jax.experimental.pallas import tpu as pltpu
from jax.sharding import Mesh
from jax.sharding import PartitionSpec as P

TILE = 64
NOCC = 200
OT = (NOCC + TILE - 1) // TILE
ZH, Y, ZL, X, CORE = 2, 8, 6, 4, 2
ALL = ("zh", "y", "zl", "x", "c")


def onehot(index_list, width):
    return (index_list[:, None] == jnp.arange(width, dtype=jnp.int32)[None, :]).astype(jnp.bfloat16)


def split_depth(where_ref, slab_ref, pattern_ref, b_ref, out):
    slab = slab_ref[where_ref[1]]
    keep = pattern_ref[where_ref[0], slab].astype(jnp.float32).astype(jnp.bfloat16)
    width = out.shape[2]
    for y in range(Y):
        out[y] = b_ref[:, y * width : (y + 1) * width] * keep


def ladder_core(core_ref, a_ref, b_ref, out, acc):
    step = pl.program_id(0)
    a = a_ref[core_ref[0]]
    half = b_ref.shape[2]

    @pl.when(step == 0)
    def _():
        acc[...] = jnp.zeros_like(acc)

    for zh in range(ZH):
        acc[:, zh * half : (zh + 1) * half] += lax.dot_general(
            a, b_ref[zh, 0], (((1,), (1,)), ((), ())), preferred_element_type=jnp.float32
        )

    @pl.when(step == ZL - 1)
    def _():
        columns = acc.shape[1] // 128
        chips = Y * X
        per = acc.shape[0] // chips
        for i in range(per):
            for k in range(columns):
                out[pl.ds(i * columns + k, chips, stride=per * columns), :] = acc[
                    i * chips : (i + 1) * chips, k * 128 : (k + 1) * 128
                ]


def per_device(amplitudes, integrals, amp_pattern, int_pattern, slab_ids, pair_window):
    zh, y, zl, x, c = (lax.axis_index(name) for name in ALL)
    block = zh * Y + y
    owner = (zl * X + x) * CORE + c
    pairs, slabs, depth = amplitudes.shape
    rows = integrals.shape[0]
    width = depth // Y
    smem = pl.BlockSpec(memory_space=pltpu.SMEM)

    ready = pl.pallas_call(
        split_depth,
        out_shape=jax.ShapeDtypeStruct((Y, rows, width), jnp.bfloat16),
        in_specs=[smem, smem, smem, pl.BlockSpec(memory_space=pltpu.VMEM)],
        out_specs=pl.BlockSpec(memory_space=pltpu.VMEM),
    )(jnp.stack([block, owner]).astype(jnp.int32), slab_ids, int_pattern, integrals.reshape(rows, depth))
    moved = lax.all_to_all(ready, "y", 0, 0, tiled=True)
    gathered = lax.all_gather(moved.reshape(Y * rows, width), ("zh", "zl"), axis=0, tiled=True)
    gathered = gathered.reshape(ZH, ZL, Y * rows, width)

    window = lax.dynamic_slice_in_dim(pair_window, (block * (ZL * X * CORE) + owner) * pairs, pairs, 1)
    occ_tile = window[0] // TILE * OT + window[1] // TILE
    picked = jnp.dot(onehot(occ_tile, amp_pattern.shape[0]), amp_pattern.astype(jnp.bfloat16))
    mask = jnp.dot(picked, onehot(slab_ids, amp_pattern.shape[1]).T)
    masked = amplitudes * mask[:, :, None]
    masked = masked.reshape(pairs, ZL, X * CORE, Y, width).transpose(3, 2, 0, 1, 4)
    masked = masked.reshape(Y * X * CORE, pairs * ZL, width)
    masked, _ = lax.optimization_barrier((masked, moved))
    swapped = lax.all_to_all(masked, ("y", "x", "c"), 0, 0, tiled=True)
    amps = swapped.reshape(Y * X, CORE, pairs, ZL, width).transpose(1, 2, 0, 3, 4)
    amps = amps.reshape(CORE, pairs * Y * X, ZL * width)

    cols = ZH * Y * rows
    lines = cols // 128
    out_rows = Y * X * pairs * lines

    def product(core, amps):
        return pl.pallas_call(
            ladder_core,
            grid=(ZL,),
            out_shape=jax.ShapeDtypeStruct((out_rows, 128), jnp.float32),
            in_specs=[
                smem,
                pl.BlockSpec((CORE, pairs * Y * X, width), lambda k: (0, 0, k)),
                pl.BlockSpec((ZH, 1, Y * rows, width), lambda k: (0, k, 0, 0)),
            ],
            out_specs=pl.BlockSpec((out_rows, 128), lambda k: (0, 0)),
            scratch_shapes=[pltpu.VMEM((pairs * Y * X, cols), jnp.float32)],
            compiler_params=pltpu.CompilerParams(
                dimension_semantics=("arbitrary",), vmem_limit_bytes=56 * 1024 * 1024
            ),
            cost_estimate=pl.CostEstimate(
                flops=2 * pairs * Y * X * cols * ZL * width,
                bytes_accessed=8 * 1024 * 1024,
                transcendentals=0,
            ),
        )(core.reshape(1).astype(jnp.int32), amps, gathered)

    other = product(1 - c, amps)
    got = lax.ppermute(other, "c", [(0, 1), (1, 0)])
    later, _ = lax.optimization_barrier((amps, other))
    mine = product(c, later)
    summed = (mine + got).reshape(Y * X, pairs * lines, 128)
    sums = lax.all_to_all(summed, ("y", "x"), 0, 0, tiled=True)
    return sums.sum(0).reshape(pairs, cols)


def solution(mesh):
    fine = Mesh(mesh.devices.reshape(ZH, Y, ZL, X, CORE), ALL)
    first = ("zh", "y", "zl", "x", "c")
    placed = (P(first, None, None), P(("zh", "y"), ("zl", "x", "c"), None), P(), P(), P(), P())
    return jax.shard_map(per_device, mesh=fine, in_specs=placed, out_specs=P(first, None), check_vma=False)
```

```python
import functools

import jax
import jax.numpy as jnp
from jax import lax
from jax.experimental import pallas as pl
from jax.experimental.pallas import tpu as pltpu
from jax.sharding import Mesh
from jax.sharding import PartitionSpec as P

TILE = 64
NOCC = 200
OT = (NOCC + TILE - 1) // TILE
ZH, Y, ZL, X, CORE = 2, 8, 6, 4, 2
ALL = ("zh", "y", "zl", "x", "c")


def onehot(index_list, width):
    return (index_list[:, None] == jnp.arange(width, dtype=jnp.int32)[None, :]).astype(jnp.bfloat16)


def split_depth(where_ref, slab_ref, pattern_ref, b_ref, out):
    slab = slab_ref[where_ref[1]]
    keep = pattern_ref[where_ref[0], slab].astype(jnp.float32).astype(jnp.bfloat16)
    width = out.shape[2]
    for y in range(Y):
        out[y] = b_ref[:, y * width : (y + 1) * width] * keep


def ladder(core_ref, a_ref, b_ref, mine_ref, other_ref, held, landed):
    core = core_ref[0]
    width = b_ref.shape[3]
    copies = [
        [
            pltpu.make_async_copy(
                b_ref.at[zh, zl], held.at[zh, :, pl.ds(zl * width, width)], landed.at[zh, zl]
            )
            for zl in range(ZL)
        ]
        for zh in range(ZH)
    ]
    for group in copies:
        for copy in group:
            copy.start()
    per = a_ref.shape[1]
    chips = Y * X
    stride = mine_ref.shape[0] // chips
    columns = stride * chips // per
    both = jnp.concatenate([a_ref[core], a_ref[1 - core]], axis=0)
    for zh, group in enumerate(copies):
        for copy in group:
            copy.wait()
        acc = lax.dot_general(
            both, held[zh], (((1,), (1,)), ((), ())), preferred_element_type=jnp.float32
        )
        tiles = acc.shape[1] // 128
        for t, out in enumerate((mine_ref, other_ref)):
            for i in range(per // chips):
                for k in range(tiles):
                    start = t * per + i * chips
                    out[pl.ds(i * columns + zh * tiles + k, chips, stride=stride), :] = acc[
                        start : start + chips, k * 128 : (k + 1) * 128
                    ]


def per_device(amplitudes, integrals, amp_pattern, int_pattern, slab_ids, pair_window):
    zh, y, zl, x, c = (lax.axis_index(name) for name in ALL)
    block = zh * Y + y
    owner = (zl * X + x) * CORE + c
    pairs, slabs, depth = amplitudes.shape
    rows = integrals.shape[0]
    width = depth // Y
    smem = pl.BlockSpec(memory_space=pltpu.SMEM)

    ready = pl.pallas_call(
        split_depth,
        out_shape=jax.ShapeDtypeStruct((Y, rows, width), jnp.bfloat16),
        in_specs=[smem, smem, smem, pl.BlockSpec(memory_space=pltpu.VMEM)],
        out_specs=pl.BlockSpec(memory_space=pltpu.VMEM),
    )(jnp.stack([block, owner]).astype(jnp.int32), slab_ids, int_pattern, integrals.reshape(rows, depth))
    moved = lax.all_to_all(ready, "y", 0, 0, tiled=True)
    gathered = lax.all_gather(moved.reshape(Y * rows, width), ("zh", "zl"), axis=0, tiled=True)
    gathered = gathered.reshape(ZH, ZL, Y * rows, width)

    window = lax.dynamic_slice_in_dim(pair_window, (block * (ZL * X * CORE) + owner) * pairs, pairs, 1)
    occ_tile = window[0] // TILE * OT + window[1] // TILE
    picked = jnp.dot(onehot(occ_tile, amp_pattern.shape[0]), amp_pattern.astype(jnp.bfloat16))
    mask = jnp.dot(picked, onehot(slab_ids, amp_pattern.shape[1]).T)
    masked = amplitudes * mask[:, :, None]
    masked = masked.reshape(pairs, ZL, X * CORE, Y, width).transpose(3, 2, 0, 1, 4)
    masked = masked.reshape(Y * X * CORE, pairs * ZL, width)
    masked, _ = lax.optimization_barrier((masked, moved))
    swapped = lax.all_to_all(masked, ("y", "x", "c"), 0, 0, tiled=True)
    amps = swapped.reshape(Y * X, CORE, pairs, ZL, width).transpose(1, 2, 0, 3, 4)
    amps = amps.reshape(CORE, pairs * Y * X, ZL * width)

    cols = ZH * Y * rows
    lines = cols // 128
    out_rows = Y * X * pairs * lines

    mine, other = pl.pallas_call(
        ladder,
        out_shape=[jax.ShapeDtypeStruct((out_rows, 128), jnp.float32)] * 2,
        in_specs=[smem, pl.BlockSpec(memory_space=pltpu.VMEM), pl.BlockSpec(memory_space=pltpu.HBM)],
        out_specs=[pl.BlockSpec(memory_space=pltpu.VMEM)] * 2,
        scratch_shapes=[
            pltpu.VMEM((ZH, Y * rows, ZL * width), jnp.bfloat16),
            pltpu.SemaphoreType.DMA((ZH, ZL)),
        ],
        compiler_params=pltpu.CompilerParams(vmem_limit_bytes=48 * 1024 * 1024),
        cost_estimate=pl.CostEstimate(
            flops=4 * pairs * Y * X * cols * ZL * width, bytes_accessed=8 * 1024 * 1024, transcendentals=0
        ),
    )(c.reshape(1).astype(jnp.int32), amps, gathered)
    got = lax.ppermute(other, "c", [(0, 1), (1, 0)])
    summed = (mine + got).reshape(Y * X, pairs * lines, 128)
    sums = lax.all_to_all(summed, ("y", "x"), 0, 0, tiled=True)
    return sums.sum(0).reshape(pairs, cols)


def solution(mesh):
    fine = Mesh(mesh.devices.reshape(ZH, Y, ZL, X, CORE), ALL)
    first = ("zh", "y", "zl", "x", "c")
    placed = (P(first, None, None), P(("zh", "y"), ("zl", "x", "c"), None), P(), P(), P(), P())
    return jax.shard_map(per_device, mesh=fine, in_specs=placed, out_specs=P(first, None), check_vma=False)
```

```python
import functools

import jax
import jax.numpy as jnp
from jax import lax
from jax.experimental import pallas as pl
from jax.experimental.pallas import tpu as pltpu
from jax.sharding import Mesh
from jax.sharding import PartitionSpec as P

TILE = 64
NOCC = 200
OT = (NOCC + TILE - 1) // TILE
ZH, Y, ZL, X, CORE = 2, 8, 6, 4, 2
RING = ZH * ZL
LANES = 128
ALL = ("zh", "y", "zl", "x", "c")


def onehot(index_list, width):
    return (index_list[:, None] == jnp.arange(width, dtype=jnp.int32)[None, :]).astype(jnp.bfloat16)


def split_depth(where_ref, slab_ref, pattern_ref, b_ref, out):
    slab = slab_ref[where_ref[1]]
    keep = pattern_ref[where_ref[0], slab].astype(jnp.float32).astype(jnp.bfloat16)
    width = out.shape[2]
    for y in range(Y):
        out[y] = b_ref[:, y * width : (y + 1) * width] * keep


def ladder(where_ref, a_ref, b_ref, *rest):
    near = rest[:RING]
    mine_ref, other_ref, held, landed, near_landed = rest[RING:]
    core, place = where_ref[0], where_ref[1]
    width = b_ref.shape[3] + LANES
    for e, ref in enumerate(near):
        spot = (place + e) % RING
        column = pl.multiple_of((spot % ZL) * width + (width - LANES), LANES)
        pltpu.make_async_copy(
            ref, held.at[spot // ZL, :, pl.ds(column, LANES)], near_landed.at[e]
        ).start()
    copies = [
        [
            pltpu.make_async_copy(
                b_ref.at[zh, zl],
                held.at[zh, :, pl.ds(zl * width, width - LANES)],
                landed.at[zh, zl],
            )
            for zl in range(ZL)
        ]
        for zh in range(ZH)
    ]
    for group in copies:
        for copy in group:
            copy.start()
    for e, ref in enumerate(near):
        pltpu.make_async_copy(ref, held.at[0, :, pl.ds(0, LANES)], near_landed.at[e]).wait()
    per = a_ref.shape[1]
    chips = Y * X
    stride = mine_ref.shape[0] // chips
    columns = stride * chips // per
    both = jnp.concatenate([a_ref[core], a_ref[1 - core]], axis=0)
    for zh, group in enumerate(copies):
        for copy in group:
            copy.wait()
        acc = lax.dot_general(
            both, held[zh], (((1,), (1,)), ((), ())), preferred_element_type=jnp.float32
        )
        tiles = acc.shape[1] // 128
        for t, out in enumerate((mine_ref, other_ref)):
            for i in range(per // chips):
                for k in range(tiles):
                    start = t * per + i * chips
                    out[pl.ds(i * columns + zh * tiles + k, chips, stride=stride), :] = acc[
                        start : start + chips, k * 128 : (k + 1) * 128
                    ]


def per_device(amplitudes, integrals, amp_pattern, int_pattern, slab_ids, pair_window):
    zh, y, zl, x, c = (lax.axis_index(name) for name in ALL)
    block = zh * Y + y
    owner = (zl * X + x) * CORE + c
    pairs, slabs, depth = amplitudes.shape
    rows = integrals.shape[0]
    width = depth // Y
    smem = pl.BlockSpec(memory_space=pltpu.SMEM)

    ready = pl.pallas_call(
        split_depth,
        out_shape=jax.ShapeDtypeStruct((Y, rows, width), jnp.bfloat16),
        in_specs=[smem, smem, smem, pl.BlockSpec(memory_space=pltpu.VMEM)],
        out_specs=pl.BlockSpec(memory_space=pltpu.VMEM),
    )(jnp.stack([block, owner]).astype(jnp.int32), slab_ids, int_pattern, integrals.reshape(rows, depth))
    moved = lax.all_to_all(ready, "y", 0, 0, tiled=True)
    moved = moved.reshape(Y * rows, width)
    gathered = lax.all_gather(moved[:, : width - LANES], ("zh", "zl"), axis=0, tiled=True)
    gathered = gathered.reshape(ZH, ZL, Y * rows, width - LANES)
    up = [(z, (z + 1) % RING) for z in range(RING)]
    down = [(z, (z - 1) % RING) for z in range(RING)]
    near = {0: moved[:, width - LANES :]}
    for step in range(RING // 2):
        near[RING - 1 - step] = lax.ppermute(near[(RING - step) % RING], ("zh", "zl"), up)
        if step + 1 < RING // 2:
            near[step + 1] = lax.ppermute(near[step], ("zh", "zl"), down)

    window = lax.dynamic_slice_in_dim(pair_window, (block * (ZL * X * CORE) + owner) * pairs, pairs, 1)
    occ_tile = window[0] // TILE * OT + window[1] // TILE
    picked = jnp.dot(onehot(occ_tile, amp_pattern.shape[0]), amp_pattern.astype(jnp.bfloat16))
    mask = jnp.dot(picked, onehot(slab_ids, amp_pattern.shape[1]).T)
    masked = amplitudes * mask[:, :, None]
    masked = masked.reshape(pairs, ZL, X * CORE, Y, width).transpose(3, 2, 0, 1, 4)
    masked = masked.reshape(Y * X * CORE, pairs * ZL, width)
    masked, _ = lax.optimization_barrier((masked, moved))
    swapped = lax.all_to_all(masked, ("y", "x", "c"), 0, 0, tiled=True)
    amps = swapped.reshape(Y * X, CORE, pairs, ZL, width).transpose(1, 2, 0, 3, 4)
    amps = amps.reshape(CORE, pairs * Y * X, ZL * width)

    cols = ZH * Y * rows
    lines = cols // 128
    out_rows = Y * X * pairs * lines

    mine, other = pl.pallas_call(
        ladder,
        out_shape=[jax.ShapeDtypeStruct((out_rows, 128), jnp.float32)] * 2,
        in_specs=[
            smem,
            pl.BlockSpec(memory_space=pltpu.VMEM),
            pl.BlockSpec(memory_space=pltpu.HBM),
        ]
        + [pl.BlockSpec(memory_space=pl.ANY)] * RING,
        out_specs=[pl.BlockSpec(memory_space=pltpu.VMEM)] * 2,
        scratch_shapes=[
            pltpu.VMEM((ZH, Y * rows, ZL * width), jnp.bfloat16),
            pltpu.SemaphoreType.DMA((ZH, ZL)),
            pltpu.SemaphoreType.DMA((RING,)),
        ],
        compiler_params=pltpu.CompilerParams(vmem_limit_bytes=48 * 1024 * 1024),
        cost_estimate=pl.CostEstimate(
            flops=4 * pairs * Y * X * cols * ZL * width, bytes_accessed=8 * 1024 * 1024, transcendentals=0
        ),
    )(
        jnp.stack([c, zh * ZL + zl]).astype(jnp.int32), amps, gathered, *[near[e] for e in range(RING)]
    )
    got = lax.ppermute(other, "c", [(0, 1), (1, 0)])
    summed = (mine + got).reshape(Y * X, pairs * lines, 128)
    sums = lax.all_to_all(summed, ("y", "x"), 0, 0, tiled=True)
    return sums.sum(0).reshape(pairs, cols)


def solution(mesh):
    fine = Mesh(mesh.devices.reshape(ZH, Y, ZL, X, CORE), ALL)
    first = ("zh", "y", "zl", "x", "c")
    placed = (P(first, None, None), P(("zh", "y"), ("zl", "x", "c"), None), P(), P(), P(), P())
    return jax.shard_map(per_device, mesh=fine, in_specs=placed, out_specs=P(first, None), check_vma=False)
```

```python
import functools

import jax
import jax.numpy as jnp
from jax import lax
from jax.experimental import pallas as pl
from jax.experimental.pallas import tpu as pltpu
from jax.sharding import Mesh
from jax.sharding import PartitionSpec as P

TILE = 64
NOCC = 200
OT = (NOCC + TILE - 1) // TILE
ZH, Y, ZL, X, CORE = 2, 8, 6, 4, 2
ALL = ("zh", "y", "zl", "x", "c")


def onehot(index_list, width):
    return (index_list[:, None] == jnp.arange(width, dtype=jnp.int32)[None, :]).astype(jnp.bfloat16)


def split_depth(where_ref, slab_ref, pattern_ref, b_ref, out):
    slab = slab_ref[where_ref[1]]
    keep = pattern_ref[where_ref[0], slab].astype(jnp.float32).astype(jnp.bfloat16)
    width = out.shape[2]
    for y in range(Y):
        out[y] = b_ref[:, y * width : (y + 1) * width] * keep


def ladder(core_ref, a_ref, b_ref, last_ref, mine_ref, other_ref, held, landed):
    core = core_ref[0]
    width = b_ref.shape[3]
    rows = (0, b_ref.shape[2], b_ref.shape[2] + last_ref.shape[2])
    copies = [
        [
            pltpu.make_async_copy(
                ref.at[zh, zl],
                held.at[zh, pl.ds(rows[n], rows[n + 1] - rows[n]), pl.ds(zl * width, width)],
                landed.at[n, zh, zl],
            )
            for n, ref in enumerate((b_ref, last_ref))
            for zl in range(ZL)
        ]
        for zh in range(ZH)
    ]
    for group in copies:
        for copy in group:
            copy.start()
    per = a_ref.shape[1]
    chips = Y * X
    stride = mine_ref.shape[0] // chips
    columns = stride * chips // per
    both = jnp.concatenate([a_ref[core], a_ref[1 - core]], axis=0)
    for zh, group in enumerate(copies):
        for copy in group:
            copy.wait()
        acc = lax.dot_general(
            both, held[zh], (((1,), (1,)), ((), ())), preferred_element_type=jnp.float32
        )
        tiles = acc.shape[1] // 128
        for t, out in enumerate((mine_ref, other_ref)):
            for i in range(per // chips):
                for k in range(tiles):
                    start = t * per + i * chips
                    out[pl.ds(i * columns + zh * tiles + k, chips, stride=stride), :] = acc[
                        start : start + chips, k * 128 : (k + 1) * 128
                    ]


def per_device(amplitudes, integrals, amp_pattern, int_pattern, slab_ids, pair_window):
    zh, y, zl, x, c = (lax.axis_index(name) for name in ALL)
    block = zh * Y + y
    owner = (zl * X + x) * CORE + c
    pairs, slabs, depth = amplitudes.shape
    rows = integrals.shape[0]
    width = depth // Y
    smem = pl.BlockSpec(memory_space=pltpu.SMEM)

    ready = pl.pallas_call(
        split_depth,
        out_shape=jax.ShapeDtypeStruct((Y, rows, width), jnp.bfloat16),
        in_specs=[smem, smem, smem, pl.BlockSpec(memory_space=pltpu.VMEM)],
        out_specs=pl.BlockSpec(memory_space=pltpu.VMEM),
    )(jnp.stack([block, owner]).astype(jnp.int32), slab_ids, int_pattern, integrals.reshape(rows, depth))
    moved = lax.all_to_all(ready, "y", 0, 0, tiled=True)
    most = moved[: Y - 1].reshape((Y - 1) * rows, width)
    gathered = lax.all_gather(most, ("zh", "zl"), axis=0, tiled=True)
    gathered = gathered.reshape(ZH, ZL, (Y - 1) * rows, width)

    window = lax.dynamic_slice_in_dim(pair_window, (block * (ZL * X * CORE) + owner) * pairs, pairs, 1)
    occ_tile = window[0] // TILE * OT + window[1] // TILE
    picked = jnp.dot(onehot(occ_tile, amp_pattern.shape[0]), amp_pattern.astype(jnp.bfloat16))
    mask = jnp.dot(picked, onehot(slab_ids, amp_pattern.shape[1]).T)
    masked = amplitudes * mask[:, :, None]
    masked = masked.reshape(pairs, ZL, X * CORE, Y, width).transpose(3, 2, 0, 1, 4)
    masked = masked.reshape(Y * X * CORE, pairs * ZL, width)
    masked, last = lax.optimization_barrier((masked, moved[Y - 1]))
    swapped = lax.all_to_all(masked, ("y", "x", "c"), 0, 0, tiled=True)
    last = lax.all_gather(last, ("zh", "zl"), axis=0, tiled=True).reshape(ZH, ZL, rows, width)
    amps = swapped.reshape(Y * X, CORE, pairs, ZL, width).transpose(1, 2, 0, 3, 4)
    amps = amps.reshape(CORE, pairs * Y * X, ZL * width)

    cols = ZH * Y * rows
    lines = cols // 128
    out_rows = Y * X * pairs * lines

    mine, other = pl.pallas_call(
        ladder,
        out_shape=[jax.ShapeDtypeStruct((out_rows, 128), jnp.float32)] * 2,
        in_specs=[
            smem,
            pl.BlockSpec(memory_space=pltpu.VMEM),
            pl.BlockSpec(memory_space=pltpu.HBM),
            pl.BlockSpec(memory_space=pl.ANY),
        ],
        out_specs=[pl.BlockSpec(memory_space=pltpu.VMEM)] * 2,
        scratch_shapes=[
            pltpu.VMEM((ZH, Y * rows, ZL * width), jnp.bfloat16),
            pltpu.SemaphoreType.DMA((2, ZH, ZL)),
        ],
        compiler_params=pltpu.CompilerParams(vmem_limit_bytes=48 * 1024 * 1024),
        cost_estimate=pl.CostEstimate(
            flops=4 * pairs * Y * X * cols * ZL * width, bytes_accessed=8 * 1024 * 1024, transcendentals=0
        ),
    )(c.reshape(1).astype(jnp.int32), amps, gathered, last)
    got = lax.ppermute(other, "c", [(0, 1), (1, 0)])
    summed = (mine + got).reshape(Y * X, pairs * lines, 128)
    sums = lax.all_to_all(summed, ("y", "x"), 0, 0, tiled=True)
    return sums.sum(0).reshape(pairs, cols)


def solution(mesh):
    fine = Mesh(mesh.devices.reshape(ZH, Y, ZL, X, CORE), ALL)
    first = ("zh", "y", "zl", "x", "c")
    placed = (P(first, None, None), P(("zh", "y"), ("zl", "x", "c"), None), P(), P(), P(), P())
    return jax.shard_map(per_device, mesh=fine, in_specs=placed, out_specs=P(first, None), check_vma=False)
```

```python
import functools

import jax
import jax.numpy as jnp
from jax import lax
from jax.experimental import pallas as pl
from jax.experimental.pallas import tpu as pltpu
from jax.sharding import Mesh
from jax.sharding import PartitionSpec as P

TILE = 64
NOCC = 200
OT = (NOCC + TILE - 1) // TILE
ZH, Y, ZL, X, CORE = 2, 8, 6, 4, 2
ALL = ("zh", "y", "zl", "x", "c")


def onehot(index_list, width):
    return (index_list[:, None] == jnp.arange(width, dtype=jnp.int32)[None, :]).astype(jnp.bfloat16)


def split_depth(slab_ref, pattern_ref, b_ref, out):
    zh, y, zl, x, c = (lax.axis_index(name) for name in ALL)
    slab = slab_ref[(zl * X + x) * CORE + c]
    keep = pattern_ref[zh * Y + y, slab].astype(jnp.float32).astype(jnp.bfloat16)
    width = out.shape[2]
    for k in range(Y):
        out[k] = b_ref[:, k * width : (k + 1) * width] * keep


def ladder(a_ref, b_ref, mine_ref, other_ref, held, landed):
    core = lax.axis_index("c")
    width = b_ref.shape[3]
    copies = [
        [
            pltpu.make_async_copy(
                b_ref.at[zh, zl], held.at[zh, :, pl.ds(zl * width, width)], landed.at[zh, zl]
            )
            for zl in range(ZL)
        ]
        for zh in range(ZH)
    ]
    for group in copies:
        for copy in group:
            copy.start()
    per = a_ref.shape[1]
    chips = Y * X
    stride = mine_ref.shape[0] // chips
    fold = per // chips
    both = a_ref[...].reshape(CORE * per, a_ref.shape[2])
    for zh, group in enumerate(copies):
        for copy in group:
            copy.wait()
        acc = lax.dot_general(
            both, held[zh], (((1,), (1,)), ((), ())), preferred_element_type=jnp.float32
        )
        tiles = acc.shape[1] // 128

        def store(outs):
            for t, out in enumerate(outs):
                for i in range(fold):
                    for k in range(tiles):
                        start = t * per + i * chips
                        out[pl.ds((zh * tiles + k) * fold + i, chips, stride=stride), :] = acc[
                            start : start + chips, k * 128 : (k + 1) * 128
                        ]

        pl.when(core == 0)(functools.partial(store, (mine_ref, other_ref)))
        pl.when(core != 0)(functools.partial(store, (other_ref, mine_ref)))


def per_device(amplitudes, integrals, amp_pattern, int_pattern, slab_ids, pair_window):
    zh, y, zl, x, c = (lax.axis_index(name) for name in ALL)
    block = zh * Y + y
    owner = (zl * X + x) * CORE + c
    pairs, slabs, depth = amplitudes.shape
    rows = integrals.shape[0]
    width = depth // Y
    smem = pl.BlockSpec(memory_space=pltpu.SMEM)

    ready = pl.pallas_call(
        split_depth,
        out_shape=jax.ShapeDtypeStruct((Y, rows, width), jnp.bfloat16),
        in_specs=[smem, smem, pl.BlockSpec(memory_space=pltpu.VMEM)],
        out_specs=pl.BlockSpec(memory_space=pltpu.VMEM),
    )(slab_ids, int_pattern, integrals.reshape(rows, depth))
    moved = lax.all_to_all(ready, "y", 0, 0, tiled=True)
    gathered = lax.all_gather(moved.reshape(Y * rows, width), ("zh", "zl"), axis=0, tiled=True)
    gathered = gathered.reshape(ZH, ZL, Y * rows, width)

    window = lax.dynamic_slice_in_dim(pair_window, (block * (ZL * X * CORE) + owner) * pairs, pairs, 1)
    occ_tile = window[0] // TILE * OT + window[1] // TILE
    picked = jnp.dot(onehot(occ_tile, amp_pattern.shape[0]), amp_pattern.astype(jnp.bfloat16))
    mask = jnp.dot(picked, onehot(slab_ids, amp_pattern.shape[1]).T)
    masked = amplitudes * mask[:, :, None]
    masked = masked.reshape(pairs, ZL, X * CORE, Y, width).transpose(3, 2, 0, 1, 4)
    masked = masked.reshape(Y * X * CORE, pairs * ZL, width)
    masked, _ = lax.optimization_barrier((masked, moved))
    swapped = lax.all_to_all(masked, ("y", "x", "c"), 0, 0, tiled=True)
    amps = swapped.reshape(Y * X, CORE, pairs, ZL, width).transpose(1, 2, 0, 3, 4)
    amps = amps.reshape(CORE, pairs * Y * X, ZL * width)

    cols = ZH * Y * rows
    lines = cols // 128
    out_rows = Y * X * pairs * lines

    mine, other = pl.pallas_call(
        ladder,
        out_shape=[jax.ShapeDtypeStruct((out_rows, 128), jnp.float32)] * 2,
        in_specs=[pl.BlockSpec(memory_space=pltpu.VMEM), pl.BlockSpec(memory_space=pltpu.HBM)],
        out_specs=[pl.BlockSpec(memory_space=pltpu.VMEM)] * 2,
        scratch_shapes=[
            pltpu.VMEM((ZH, Y * rows, ZL * width), jnp.bfloat16),
            pltpu.SemaphoreType.DMA((ZH, ZL)),
        ],
        compiler_params=pltpu.CompilerParams(vmem_limit_bytes=48 * 1024 * 1024),
        cost_estimate=pl.CostEstimate(
            flops=4 * pairs * Y * X * cols * ZL * width, bytes_accessed=8 * 1024 * 1024, transcendentals=0
        ),
    )(amps, gathered)
    got = lax.ppermute(other, "c", [(0, 1), (1, 0)])
    summed = (mine + got).reshape(Y * X, pairs * lines, 128)
    sums = lax.all_to_all(summed, ("y", "x"), 0, 0, tiled=True)
    return sums.sum(0).reshape(lines, pairs, 128).transpose(1, 0, 2).reshape(pairs, cols)


def solution(mesh):
    fine = Mesh(mesh.devices.reshape(ZH, Y, ZL, X, CORE), ALL)
    first = ("zh", "y", "zl", "x", "c")
    placed = (P(first, None, None), P(("zh", "y"), ("zl", "x", "c"), None), P(), P(), P(), P())
    return jax.shard_map(per_device, mesh=fine, in_specs=placed, out_specs=P(first, None), check_vma=False)
```

```python
import jax
import jax.numpy as jnp
from jax import lax
from jax.experimental import pallas as pl
from jax.experimental.pallas import tpu as pltpu
from jax.sharding import Mesh
from jax.sharding import PartitionSpec as P

TILE = 64
NOCC = 200
OT = (NOCC + TILE - 1) // TILE
ZH, Y, ZL, X, CORE = 2, 8, 6, 4, 2
ALL = ("zh", "y", "zl", "x", "c")


def onehot(index_list, width):
    return (index_list[:, None] == jnp.arange(width, dtype=jnp.int32)[None, :]).astype(jnp.bfloat16)


def split_depth(slab_ref, pattern_ref, b_ref, out):
    zh, y, zl, x, c = (lax.axis_index(name) for name in ALL)
    slab = slab_ref[(zl * X + x) * CORE + c]
    keep = pattern_ref[zh * Y + y, slab].astype(jnp.float32).astype(jnp.bfloat16)
    width = out.shape[2]
    for k in range(Y):
        out[k] = b_ref[:, k * width : (k + 1) * width] * keep


def ladder(a_ref, b_ref, mine_ref, other_ref, held, sums, landed):
    core = lax.axis_index("c")
    width = b_ref.shape[3]
    copies = [
        [
            pltpu.make_async_copy(
                b_ref.at[zh, zl], held.at[zh, :, pl.ds(zl * width, width)], landed.at[zh, zl]
            )
            for zl in range(ZL)
        ]
        for zh in range(ZH)
    ]
    for group in copies:
        for copy in group:
            copy.start()
    per = a_ref.shape[1]
    chips = Y * X
    stride = mine_ref.shape[0] // chips
    fold = per // chips
    both = a_ref[...].reshape(CORE * per, a_ref.shape[2])
    for zh, group in enumerate(copies):
        for copy in group:
            copy.wait()
        sums[...] = lax.dot_general(
            both, held[zh], (((1,), (1,)), ((), ())), preferred_element_type=jnp.float32
        )
        tiles = sums.shape[1] // 128
        for out, side in ((mine_ref, core), (other_ref, 1 - core)):
            for i in range(fold):
                picked = pl.ds(pl.multiple_of(side * per + i * chips, chips), chips)
                for k in range(tiles):
                    out[pl.ds((zh * tiles + k) * fold + i, chips, stride=stride), :] = sums[
                        picked, k * 128 : (k + 1) * 128
                    ]


def per_device(amplitudes, integrals, amp_pattern, int_pattern, slab_ids, pair_window):
    zh, y, zl, x, c = (lax.axis_index(name) for name in ALL)
    block = zh * Y + y
    owner = (zl * X + x) * CORE + c
    pairs, slabs, depth = amplitudes.shape
    rows = integrals.shape[0]
    width = depth // Y
    smem = pl.BlockSpec(memory_space=pltpu.SMEM)

    ready = pl.pallas_call(
        split_depth,
        out_shape=jax.ShapeDtypeStruct((Y, rows, width), jnp.bfloat16),
        in_specs=[smem, smem, pl.BlockSpec(memory_space=pltpu.VMEM)],
        out_specs=pl.BlockSpec(memory_space=pltpu.VMEM),
    )(slab_ids, int_pattern, integrals.reshape(rows, depth))
    moved = lax.all_to_all(ready, "y", 0, 0, tiled=True)
    gathered = lax.all_gather(moved.reshape(Y * rows, width), ("zh", "zl"), axis=0, tiled=True)
    gathered = gathered.reshape(ZH, ZL, Y * rows, width)

    window = lax.dynamic_slice_in_dim(pair_window, (block * (ZL * X * CORE) + owner) * pairs, pairs, 1)
    occ_tile = window[0] // TILE * OT + window[1] // TILE
    picked = jnp.dot(onehot(occ_tile, amp_pattern.shape[0]), amp_pattern.astype(jnp.bfloat16))
    mask = jnp.dot(picked, onehot(slab_ids, amp_pattern.shape[1]).T)
    masked = amplitudes * mask[:, :, None]
    masked = masked.reshape(pairs, ZL, X * CORE, Y, width).transpose(3, 2, 0, 1, 4)
    masked = masked.reshape(Y * X * CORE, pairs * ZL, width)
    masked, _ = lax.optimization_barrier((masked, moved))
    swapped = lax.all_to_all(masked, ("y", "x", "c"), 0, 0, tiled=True)
    amps = swapped.reshape(Y * X, CORE, pairs, ZL, width).transpose(1, 2, 0, 3, 4)
    amps = amps.reshape(CORE, pairs * Y * X, ZL * width)

    cols = ZH * Y * rows
    lines = cols // 128
    out_rows = Y * X * pairs * lines

    mine, other = pl.pallas_call(
        ladder,
        out_shape=[jax.ShapeDtypeStruct((out_rows, 128), jnp.float32)] * 2,
        in_specs=[pl.BlockSpec(memory_space=pltpu.VMEM), pl.BlockSpec(memory_space=pltpu.HBM)],
        out_specs=[pl.BlockSpec(memory_space=pltpu.VMEM)] * 2,
        scratch_shapes=[
            pltpu.VMEM((ZH, Y * rows, ZL * width), jnp.bfloat16),
            pltpu.VMEM((CORE * pairs * Y * X, Y * rows), jnp.float32),
            pltpu.SemaphoreType.DMA((ZH, ZL)),
        ],
        compiler_params=pltpu.CompilerParams(vmem_limit_bytes=48 * 1024 * 1024),
        cost_estimate=pl.CostEstimate(
            flops=4 * pairs * Y * X * cols * ZL * width, bytes_accessed=8 * 1024 * 1024, transcendentals=0
        ),
    )(amps, gathered)
    got = lax.ppermute(other, "c", [(0, 1), (1, 0)])
    summed = (mine + got).reshape(Y * X, pairs * lines, 128)
    sums = lax.all_to_all(summed, ("y", "x"), 0, 0, tiled=True)
    return sums.sum(0).reshape(lines, pairs, 128).transpose(1, 0, 2).reshape(pairs, cols)


def solution(mesh):
    fine = Mesh(mesh.devices.reshape(ZH, Y, ZL, X, CORE), ALL)
    first = ("zh", "y", "zl", "x", "c")
    placed = (P(first, None, None), P(("zh", "y"), ("zl", "x", "c"), None), P(), P(), P(), P())
    return jax.shard_map(per_device, mesh=fine, in_specs=placed, out_specs=P(first, None), check_vma=False)
```

```python
import jax
import jax.numpy as jnp
from jax import lax
from jax.experimental import pallas as pl
from jax.experimental.pallas import tpu as pltpu
from jax.sharding import Mesh
from jax.sharding import PartitionSpec as P

TILE = 64
NOCC = 200
OT = (NOCC + TILE - 1) // TILE
ZH, Y, ZL, X, CORE = 2, 8, 6, 4, 2
ALL = ("zh", "y", "zl", "x", "c")


def onehot(index_list, width):
    return (index_list[:, None] == jnp.arange(width, dtype=jnp.int32)[None, :]).astype(jnp.bfloat16)


def split_depth(slab_ref, pattern_ref, b_ref, out):
    zh, y, zl, x, c = (lax.axis_index(name) for name in ALL)
    slab = slab_ref[(zl * X + x) * CORE + c]
    keep = pattern_ref[zh * Y + y, slab].astype(jnp.float32).astype(jnp.bfloat16)
    width = out.shape[2]
    for k in range(Y):
        out[k] = b_ref[:, k * width : (k + 1) * width] * keep


def ladder(core_ref, a_ref, b_ref, mine_ref, other_ref, held, sums, landed):
    core = core_ref[0]
    width = b_ref.shape[3]
    copies = [
        [
            pltpu.make_async_copy(
                b_ref.at[zh, zl], held.at[zh, :, pl.ds(zl * width, width)], landed.at[zh, zl]
            )
            for zl in range(ZL)
        ]
        for zh in range(ZH)
    ]
    for group in copies:
        for copy in group:
            copy.start()
    per = a_ref.shape[1]
    chips = Y * X
    stride = mine_ref.shape[0] // chips
    fold = per // chips
    both = a_ref[...].reshape(CORE * per, a_ref.shape[2])
    for zh, group in enumerate(copies):
        for copy in group:
            copy.wait()
        sums[...] = lax.dot_general(
            both, held[zh], (((1,), (1,)), ((), ())), preferred_element_type=jnp.float32
        )
        tiles = sums.shape[1] // 128
        for out, side in ((mine_ref, core), (other_ref, 1 - core)):
            for i in range(fold):
                picked = pl.ds(pl.multiple_of(side * per + i * chips, chips), chips)
                for k in range(tiles):
                    out[pl.ds((zh * tiles + k) * fold + i, chips, stride=stride), :] = sums[
                        picked, k * 128 : (k + 1) * 128
                    ]


def per_device(amplitudes, integrals, amp_pattern, int_pattern, slab_ids, pair_window):
    zh, y, zl, x, c = (lax.axis_index(name) for name in ALL)
    block = zh * Y + y
    owner = (zl * X + x) * CORE + c
    pairs, slabs, depth = amplitudes.shape
    rows = integrals.shape[0]
    width = depth // Y
    smem = pl.BlockSpec(memory_space=pltpu.SMEM)

    ready = pl.pallas_call(
        split_depth,
        out_shape=jax.ShapeDtypeStruct((Y, rows, width), jnp.bfloat16),
        in_specs=[smem, smem, pl.BlockSpec(memory_space=pltpu.VMEM)],
        out_specs=pl.BlockSpec(memory_space=pltpu.VMEM),
        compiler_params=pltpu.CompilerParams(vmem_limit_bytes=8 * 1024 * 1024),
    )(slab_ids, int_pattern, integrals.reshape(rows, depth))
    moved = lax.all_to_all(ready, "y", 0, 0, tiled=True)
    gathered = lax.all_gather(moved.reshape(Y * rows, width), ("zh", "zl"), axis=0, tiled=True)
    gathered = gathered.reshape(ZH, ZL, Y * rows, width)

    window = lax.dynamic_slice_in_dim(pair_window, (block * (ZL * X * CORE) + owner) * pairs, pairs, 1)
    occ_tile = window[0] // TILE * OT + window[1] // TILE
    picked = jnp.dot(onehot(occ_tile, amp_pattern.shape[0]), amp_pattern.astype(jnp.bfloat16))
    mask = jnp.dot(picked, onehot(slab_ids, amp_pattern.shape[1]).T)
    masked = amplitudes * mask[:, :, None]
    masked = masked.reshape(pairs, ZL, X * CORE, Y, width).transpose(3, 2, 0, 1, 4)
    masked = masked.reshape(Y * X * CORE, pairs * ZL, width)
    masked, _ = lax.optimization_barrier((masked, moved))
    swapped = lax.all_to_all(masked, ("y", "x", "c"), 0, 0, tiled=True)
    amps = swapped.reshape(Y * X, CORE, pairs, ZL, width).transpose(1, 2, 0, 3, 4)
    amps = amps.reshape(CORE, pairs * Y * X, ZL * width)

    cols = ZH * Y * rows
    lines = cols // 128
    out_rows = Y * X * pairs * lines

    mine, other = pl.pallas_call(
        ladder,
        out_shape=[jax.ShapeDtypeStruct((out_rows, 128), jnp.float32)] * 2,
        in_specs=[smem, pl.BlockSpec(memory_space=pltpu.VMEM), pl.BlockSpec(memory_space=pltpu.HBM)],
        out_specs=[pl.BlockSpec(memory_space=pltpu.VMEM)] * 2,
        scratch_shapes=[
            pltpu.VMEM((ZH, Y * rows, ZL * width), jnp.bfloat16),
            pltpu.VMEM((CORE * pairs * Y * X, Y * rows), jnp.float32),
            pltpu.SemaphoreType.DMA((ZH, ZL)),
        ],
        compiler_params=pltpu.CompilerParams(vmem_limit_bytes=48 * 1024 * 1024),
        cost_estimate=pl.CostEstimate(
            flops=4 * pairs * Y * X * cols * ZL * width, bytes_accessed=8 * 1024 * 1024, transcendentals=0
        ),
    )(c.reshape(1).astype(jnp.int32), amps, gathered)
    got = lax.ppermute(other, "c", [(0, 1), (1, 0)])
    summed = (mine + got).reshape(Y * X, pairs * lines, 128)
    sums = lax.all_to_all(summed, ("y", "x"), 0, 0, tiled=True)
    return sums.sum(0).reshape(lines, pairs, 128).transpose(1, 0, 2).reshape(pairs, cols)


def solution(mesh):
    fine = Mesh(mesh.devices.reshape(ZH, Y, ZL, X, CORE), ALL)
    first = ("zh", "y", "zl", "x", "c")
    placed = (P(first, None, None), P(("zh", "y"), ("zl", "x", "c"), None), P(), P(), P(), P())
    return jax.shard_map(per_device, mesh=fine, in_specs=placed, out_specs=P(first, None), check_vma=False)
```
